32 devices in a mesh: parts: 2 (over y), latent: 4 (over z), tok: 2 (over x), sub: 2 (over core).
Axes of the slice: x: 2, y: 2, z: 4, core: 2. Of those that a mesh axis runs over, the one named last changes fastest.
Arguments:
- resid: bfloat16 [64, 3584], P(('parts', 'latent', 'tok'), 'sub'), parts along dimension 0, may hold values from -6 to 6
- enc_weight: bfloat16 [3584, 65536], P('sub', ('latent', 'tok')), may hold values from -0.09375 to 0.09375
- enc_bias: float32 [65536], P(('latent', 'tok')), may hold values from -3 to 3
- dec_weight: bfloat16 [65536, 3584], P(('latent', 'tok'), 'sub'), may hold values from -0.0625 to 0.0625
- dec_bias: float32 [3584], P('sub'), may hold values from -3 to 3
- spans: int32 [16, 32], P('parts'), parts along dimension 0, may hold values from 0 to 1, as said below
- owners: int32 [16], P('parts'), parts along dimension 0, may hold values from 0 to 1, as said below
Outputs:
- recon: bfloat16 [64, 3584], P(('parts', 'latent', 'tok'), 'sub'), parts along dimension 0
- owned: bfloat16 [24, 65536], P(('parts', 'tok'), 'latent'), parts along dimension 0
The draws below stay inside these ranges and needn't reach their ends.
There are 2 independent parts, one for each index of `parts`. The reference program is written for one: setup_inputs(seed, part) draws one part's arguments, and reference() takes and returns one part's arrays. A program takes and returns all parts, laid end to end along the dimension named above; an argument that names none is the same for every part. Nothing has to cross between parts.
Inputs may be any that keep to these rules, and one draw needn't show every extreme that they name: `spans`: each column holds exactly one 1; each document's ones form one contiguous run of at least one row, documents in order. `owners`: no owner holds more than 6 documents, and one owner holds exactly 6.
All inputs are finite; a program needn't handle non-finite values.
Results may differ from the reference program's by a relative error of at most 0.0055.
Values may be sent and summed in bfloat16 or wider, within the bound.
A program may use at most 128 MiB of HBM per device.

```python
import jax
import jax.numpy as jnp

D = 3584
LAT = 65536
DOC_OWN = 4
ROWS = 32
NDOC = 8
CAP = 6
N_TOK = 2


def draw_spans(key, part):
    key = jax.random.fold_in(key, 11)
    order = jax.random.permutation(key, ROWS - 1)[:NDOC - 1] + 1
    cuts = jnp.sort(order.astype(jnp.int32))
    places = jnp.arange(ROWS, dtype=jnp.int32)
    docids = jnp.sum((cuts[None, :] <= places[:, None]).astype(jnp.int32), axis=1)
    return (docids[None, :] == jnp.arange(NDOC, dtype=jnp.int32)[:, None]).astype(jnp.int32)


def draw_owners(key, part):
    key = jax.random.fold_in(key, 7)
    first_key, second_key = jax.random.split(key)
    owner_count = NDOC // DOC_OWN
    busiest = jax.random.randint(first_key, (), 0, owner_count).astype(jnp.int32)
    others = jnp.arange(NDOC - CAP, dtype=jnp.int32) % max(owner_count - 1, 1)
    others = jnp.where(others >= busiest, others + 1, others)
    listed = jnp.concatenate([jnp.full((CAP,), 1, jnp.int32) * busiest, others]).astype(jnp.int32)
    shuffle = jax.random.permutation(second_key, NDOC)
    return listed[shuffle]


def spiked(result, own_key, source, target, parts, factor):
    owner, partner = [(jnp.arange(result.shape[axis_at]) // (result.shape[axis_at] // parts)).reshape([-1 if axis == axis_at else 1 for axis in range(result.ndim)]) for axis_at in (source, target)]
    chosen = jax.random.permutation(own_key, parts)[partner]
    strong = (owner == chosen) | (owner == (partner + parts // 2) % parts)
    return jnp.where(strong, factor * result, result)


def steps_of(own_key, dims, pieces, least, high):
    def one(position, parts):
        steps = jax.random.uniform(jax.random.fold_in(jax.random.fold_in(own_key, 6), position), (parts,), jnp.float32, least / len(pieces), high / len(pieces))
        return jnp.repeat(jnp.exp(steps), dims[position] // parts).reshape((-1,) + (1,) * (len(dims) - position - 1))

    loudness = one(*pieces[0])
    for cut in pieces[1:]:
        loudness = loudness * one(*cut)
    return loudness


def bell_draw(rng, extent, width, most, shards=(), kind=jnp.bfloat16):
    loudness = steps_of(rng, extent, shards, -0.22, 0.18) if shards else 1.0
    array = jax.random.normal(rng, extent, jnp.float32) * width * loudness
    return jnp.minimum(jnp.maximum(array, -most), most).astype(kind)


def bell_draw_with(rng, shape, scale, limit, shards, heavy, kind=jnp.bfloat16):
    values = scale * jax.random.normal(rng, shape, jnp.float32)
    if shards:
        values = values * steps_of(rng, shape, shards, -0.22, 0.18)
    return jnp.clip(spiked(values, jax.random.fold_in(rng, 3), *heavy), -limit, limit).astype(kind)


def setup_inputs(seed: int = 0, part: int = 0) -> dict:
    splits = jax.random.split(jax.random.key(seed), 8)
    part_splits = jax.random.split(jax.random.fold_in(splits[7], part), 8)
    resid = bell_draw(part_splits[0], (ROWS, D), 1.0, 6.0, ((0, 8), (1, 2)))
    enc_weight = bell_draw(splits[1], (D, LAT), D ** -0.5, 0.09375, ((0, 2), (1, 8)))
    enc_bias = bell_draw(splits[2], (LAT,), 0.5, 3.0, ((0, 8),), jnp.float32)
    dec_weight = bell_draw_with(splits[3], (LAT, D), (LAT // 4) ** -0.5, 0.0625, ((0, 8), (1, 2)), (0, 1, 8, 2.0))
    dec_bias = bell_draw(splits[4], (D,), 0.5, 3.0, ((0, 2),), jnp.float32)
    spans = draw_spans(jax.random.fold_in(jax.random.fold_in(splits[7], part), 71), part)
    owners = draw_owners(jax.random.fold_in(jax.random.fold_in(splits[7], part), 71), part)
    return dict(resid=resid, enc_weight=enc_weight, enc_bias=enc_bias, dec_weight=dec_weight, dec_bias=dec_bias, spans=spans, owners=owners)


def reference(resid, enc_weight, enc_bias, dec_weight, dec_bias, spans, owners):
    centered = (resid.astype(jnp.float32) - dec_bias).astype(jnp.bfloat16)
    pre = jnp.dot(centered, enc_weight, preferred_element_type=jnp.float32) + enc_bias
    acts = jnp.maximum(pre, 0.0).astype(jnp.bfloat16)
    recon = (jnp.dot(acts, dec_weight, preferred_element_type=jnp.float32) + dec_bias).astype(jnp.bfloat16)
    counts = jnp.sum(spans, axis=1).astype(jnp.float32)
    pooled = (jnp.dot(spans.astype(jnp.bfloat16), acts, preferred_element_type=jnp.float32) / counts[:, None]).astype(jnp.bfloat16)
    hits = (owners[:, None] == jnp.arange(N_TOK, dtype=jnp.int32)[None, :]).astype(jnp.int32)
    before = jnp.cumsum(hits, axis=0) - hits
    slots = jnp.sum(before * hits, axis=1)
    target = owners * CAP + slots
    select = (target[None, :] == jnp.arange(N_TOK * CAP, dtype=jnp.int32)[:, None]).astype(jnp.bfloat16)
    owned = jnp.dot(select, pooled, preferred_element_type=jnp.float32).astype(jnp.bfloat16)
    return recon, owned
```

```python
import functools

import jax
import jax.numpy as jnp
from jax import lax
from jax.experimental import pallas as pl
from jax.experimental.pallas import tpu as pltpu
from jax.sharding import PartitionSpec as P

CAP = 6
PAD = 8
MESH = pl.DeviceIdType.MESH
BF16 = jnp.bfloat16
F32 = jnp.float32


def chunked(total, step):
    return [(at, min(step, total - at)) for at in range(0, total, step)]


def kernel(
    sizes, enc_parts, dec_parts,
    resid, enc_hbm, enc_bias, dec_hbm, dec_bias, spans, owners,
    recon, owned,
    wenc, wdec, xg, xf, x2, mg, pe, pr, acts,
    ysend, yown, yrecv, bsend, bown, brecv, csend, cown, crecv, psend, precv,
    wenc_sem, wdec_sem, gz_sem, gy_sem, gx_sem, m_sem, e_sem, a_sem, b_sem, c_sem, p_sem,
):
    n_p, n_l, n_t = sizes
    p, l, t, s = (lax.axis_index(name) for name in ("parts", "latent", "tok", "sub"))
    rows = resid.shape[0]
    half = acts.shape[1]
    total_rows = n_p * n_l * n_t * rows
    part_rows = n_l * n_t * rows

    def at(dp=0, dl=0, dt=0, ds=0):
        return (
            lax.rem(p + dp, n_p), lax.rem(l + dl, n_l), lax.rem(t + dt, n_t), lax.rem(s + ds, 2)
        )

    sent = []

    def send(src, dst, sems, index, device):
        copy = pltpu.make_async_remote_copy(
            src_ref=src, dst_ref=dst, send_sem=sems.at[(0,) + index],
            recv_sem=sems.at[(1,) + index], device_id=device, device_id_type=MESH,
        )
        copy.start()
        sent.append(copy)
        return copy

    base = pl.multiple_of(p * half, half)
    enc_copies = []
    for j, (start, width) in enumerate(enc_parts):
        copy = pltpu.make_async_copy(
            enc_hbm.at[:, pl.ds(pl.multiple_of(base + start, 128), width)],
            wenc.at[:, pl.ds(start, width)], wenc_sem.at[j],
        )
        copy.start()
        enc_copies.append(copy)

    barrier = pltpu.get_barrier_semaphore()
    peers = [at(ds=1)]
    peers += [at(dl=k) for k in range(1, n_l)]
    peers += [at(dp=a, dt=b) for a in range(n_p) for b in range(n_t) if a or b]
    for peer in peers:
        pl.semaphore_signal(barrier, inc=1, device_id=peer, device_id_type=MESH)

    xg[t, p, l] = (resid[...].astype(F32) - dec_bias[...]).astype(BF16)

    docs = spans.shape[0]
    row_i = lax.broadcasted_iota(jnp.int32, (docs, docs), 0)
    col_i = lax.broadcasted_iota(jnp.int32, (docs, docs), 1)
    across = jnp.broadcast_to(owners[...], (docs, docs))
    down = jnp.sum(jnp.where(row_i == col_i, across, 0), axis=1, keepdims=True)
    same = jnp.where((down == across) & (row_i < col_i), 1, 0)
    slots = jnp.sum(same, axis=0, keepdims=True)
    target = owners[...] * PAD + slots
    select = target == lax.broadcasted_iota(jnp.int32, (n_t * PAD, docs), 0)
    member = jnp.dot(
        jnp.where(select, 1.0, 0.0).astype(BF16), spans[...].astype(F32).astype(BF16),
        preferred_element_type=F32,
    )
    place = lax.broadcasted_iota(jnp.int32, (part_rows, total_rows), 1)
    source = lax.broadcasted_iota(jnp.int32, (part_rows, total_rows), 0)
    r_at = lax.rem(place, rows)
    l_at = lax.rem(lax.div(place, rows), n_l)
    p_at = lax.rem(lax.div(place, rows * n_l), n_p)
    t_at = lax.div(place, rows * n_l * n_p)
    wanted = jnp.where(p_at == p, (l_at * n_t + t_at) * rows + r_at, -1)
    mg[p] = jnp.dot(
        member.astype(BF16), jnp.where(source == wanted, 1.0, 0.0).astype(BF16),
        preferred_element_type=F32,
    )

    pl.semaphore_wait(barrier, len(peers))

    copies = [
        send(xg.at[t, p, l], xg.at[t, p, l], gz_sem, (k - 1,), at(dl=k)) for k in range(1, n_l)
    ]
    m_copies = [send(mg.at[p], mg.at[p], m_sem, (k - 1,), at(dp=k)) for k in range(1, n_p)]
    dec_copies = []
    for j, (start, width) in enumerate(dec_parts):
        copy = pltpu.make_async_copy(
            dec_hbm.at[pl.ds(base, half), pl.ds(start, width)],
            wdec.at[:, pl.ds(start, width)], wdec_sem.at[j],
        )
        copy.start()
        dec_copies.append(copy)
    for copy in copies:
        copy.wait_recv()
    y_copies = [send(xg.at[t, p], xg.at[t, p], gy_sem, (k - 1,), at(dp=k)) for k in range(1, n_p)]
    x_copies = [
        send(xg.at[t, p], xg.at[t, p], gx_sem, (0, k - 1), at(dt=k)) for k in range(1, n_t)
    ]
    for m, copy in enumerate(y_copies, 1):
        copy.wait_recv()
        came = lax.rem(p + n_p - m, n_p)
        x_copies += [
            send(xg.at[t, came], xg.at[t, came], gx_sem, (m, k - 1), at(dt=k))
            for k in range(1, n_t)
        ]
    for copy in x_copies:
        copy.wait_recv()
    block = 0
    for a in range(n_t):
        for b in range(n_p):
            for c in range(n_l):
                xf[pl.ds(block * rows, rows), :] = xg[a, b, c].astype(F32)
                block += 1
    x2[...] = xf[...].astype(BF16)

    e_copies = []
    for j, (start, width) in enumerate(enc_parts):
        cols = pl.ds(start, width)
        enc_copies[j].wait()
        pe[:, cols] = jnp.dot(x2[...], wenc[:, cols], preferred_element_type=F32)
        e_copies.append(send(pe.at[:, cols], pr.at[:, cols], e_sem, (j,), at(ds=1)))

    def make_acts(j):
        start, width = enc_parts[j]
        cols = pl.ds(start, width)
        e_copies[j].wait_recv()
        bias = enc_bias[:, pl.ds(pl.multiple_of(base + start, 128), width)]
        acts[:, cols] = jnp.maximum(pe[:, cols] + pr[:, cols] + bias, 0.0).astype(BF16)

    a_copies, b_copies, c_copies = {}, {}, {}

    def decode(c):
        start, width = dec_parts[c]
        cols = pl.ds(start, width)
        dec_copies[c].wait()
        if c == 0:
            y = None
            for j, (k0, kw) in enumerate(enc_parts):
                make_acts(j)
                term = jnp.dot(
                    acts[:, pl.ds(k0, kw)], wdec[pl.ds(k0, kw), cols], preferred_element_type=F32
                )
                y = term if y is None else y + term
        else:
            y = jnp.dot(acts[...], wdec[:, cols], preferred_element_type=F32)
        tall = total_rows // n_t
        for a in range(n_t):
            piece = y[a * tall:(a + 1) * tall]
            ysend[a, :, cols] = piece.astype(BF16)
            yown[a, :, cols] = piece
        a_copies[c] = []
        for k in range(1, n_t):
            peer = at(dt=k)
            a_copies[c].append(
                send(ysend.at[peer[2], :, cols], yrecv.at[k - 1, :, cols], a_sem, (c, k - 1), peer)
            )

    def sum_x(c):
        start, width = dec_parts[c]
        cols = pl.ds(start, width)
        total = yown[t, :, cols]
        for k, copy in enumerate(a_copies[c]):
            copy.wait_recv()
            total += yrecv[k, :, cols].astype(F32)
        tall = total_rows // (n_t * n_p)
        for a in range(n_p):
            piece = total[a * tall:(a + 1) * tall]
            bsend[a, :, cols] = piece.astype(BF16)
            bown[a, :, cols] = piece
        b_copies[c] = []
        for k in range(1, n_p):
            peer = at(dp=k)
            b_copies[c].append(
                send(bsend.at[peer[0], :, cols], brecv.at[k - 1, :, cols], b_sem, (c, k - 1), peer)
            )

    def sum_y(c):
        start, width = dec_parts[c]
        cols = pl.ds(start, width)
        total = bown[p, :, cols]
        for k, copy in enumerate(b_copies[c]):
            copy.wait_recv()
            total += brecv[k, :, cols].astype(F32)
        for a in range(n_l):
            piece = total[a * rows:(a + 1) * rows]
            csend[a, :, cols] = piece.astype(BF16)
            cown[a, :, cols] = piece
        c_copies[c] = []
        for k in range(1, n_l):
            peer = at(dl=k)
            c_copies[c].append(
                send(csend.at[peer[1], :, cols], crecv.at[k - 1, :, cols], c_sem, (c, k - 1), peer)
            )

    def sum_z(c):
        start, width = dec_parts[c]
        cols = pl.ds(start, width)
        total = cown[l, :, cols]
        for k, copy in enumerate(c_copies[c]):
            copy.wait_recv()
            total += crecv[k, :, cols].astype(F32)
        recon[:, cols] = (total + dec_bias[:, cols]).astype(BF16)

    def pool():
        for copy in m_copies:
            copy.wait_recv()
        spread = jnp.concatenate([mg[a] for a in range(n_p)], axis=0)
        counts = jnp.maximum(jnp.sum(spread, axis=1, keepdims=True), 1.0)
        pooled = jnp.dot(spread.astype(BF16), acts[...], preferred_element_type=F32) / counts
        for a in range(n_p * n_t):
            psend[a] = pooled[a * PAD:a * PAD + CAP].astype(BF16)
        mine = p * n_t + t
        precv[mine] = psend[mine]
        copies = []
        for a in range(n_p):
            for b in range(n_t):
                if a or b:
                    peer = at(dp=a, dt=b)
                    copies.append(
                        send(psend.at[peer[0] * n_t + peer[2]], precv.at[mine], p_sem, (a, b), peer)
                    )
        return copies

    steps = len(dec_parts)
    pool_copies = []
    for c in range(steps + 3):
        if c < steps:
            decode(c)
        if c == 0:
            pool_copies = pool()
        if 0 <= c - 1 < steps:
            sum_x(c - 1)
        if 0 <= c - 2 < steps:
            sum_y(c - 2)
        if c == steps:
            for copy in pool_copies:
                copy.wait_recv()
            for a in range(n_p):
                for b in range(n_t):
                    owned[:, pl.ds((b * n_p + a) * half, half)] = precv[a * n_t + b]
        if 0 <= c - 3 < steps:
            sum_z(c - 3)
    for copy in sent:
        copy.wait_send()


def per_device(sizes, resid, enc_weight, enc_bias, dec_weight, dec_bias, spans, owners):
    n_p, n_l, n_t = sizes
    rows, width = resid.shape
    half = enc_weight.shape[1] // n_p
    total = rows * n_p * n_l * n_t
    enc_parts = chunked(half, 1024)
    dec_parts = chunked(width, 512)
    vmem = pl.BlockSpec(memory_space=pltpu.VMEM)
    hbm = pl.BlockSpec(memory_space=pl.ANY)
    dma = pltpu.SemaphoreType.DMA
    x_rows, y_rows = total // n_t, total // (n_t * n_p)
    more = lambda n: max(n - 1, 1)
    steps = len(dec_parts)
    return pl.pallas_call(
        functools.partial(kernel, sizes, enc_parts, dec_parts),
        out_shape=(
            jax.ShapeDtypeStruct((rows, width), BF16),
            jax.ShapeDtypeStruct((CAP, half * n_p * n_t), BF16),
        ),
        in_specs=[vmem, hbm, vmem, hbm, vmem, vmem, vmem],
        out_specs=(vmem, vmem),
        scratch_shapes=[
            pltpu.VMEM((width, half), BF16),
            pltpu.VMEM((half, width), BF16),
            pltpu.VMEM((n_t, n_p, n_l, rows, width), BF16),
            pltpu.VMEM((total, width), F32),
            pltpu.VMEM((total, width), BF16),
            pltpu.VMEM((n_p, n_t * PAD, total), F32),
            pltpu.VMEM((total, half), F32),
            pltpu.VMEM((total, half), F32),
            pltpu.VMEM((total, half), BF16),
            pltpu.VMEM((n_t, x_rows, width), BF16),
            pltpu.VMEM((n_t, x_rows, width), F32),
            pltpu.VMEM((more(n_t), x_rows, width), BF16),
            pltpu.VMEM((n_p, y_rows, width), BF16),
            pltpu.VMEM((n_p, y_rows, width), F32),
            pltpu.VMEM((more(n_p), y_rows, width), BF16),
            pltpu.VMEM((n_l, rows, width), BF16),
            pltpu.VMEM((n_l, rows, width), F32),
            pltpu.VMEM((more(n_l), rows, width), BF16),
            pltpu.VMEM((n_p * n_t, CAP, half), BF16),
            pltpu.VMEM((n_p * n_t, CAP, half), BF16),
            dma((len(enc_parts),)),
            dma((steps,)),
            dma((2, more(n_l))),
            dma((2, more(n_p))),
            dma((2, n_p, more(n_t))),
            dma((2, more(n_p))),
            dma((2, len(enc_parts))),
            dma((2, steps, more(n_t))),
            dma((2, steps, more(n_p))),
            dma((2, steps, more(n_l))),
            dma((2, n_p, n_t)),
        ],
        compiler_params=pltpu.CompilerParams(
            collective_id=0, has_side_effects=True, vmem_limit_bytes=58 * 1024 * 1024
        ),
        cost_estimate=pl.CostEstimate(
            flops=4 * total * width * half, bytes_accessed=4 * width * half, transcendentals=0
        ),
    )(
        resid, enc_weight, enc_bias[None, :], dec_weight, dec_bias[None, :], spans, owners[None, :]
    )


def solution(mesh):
    placed = (
        P(("parts", "latent", "tok"), "sub"),
        P("sub", ("latent", "tok")),
        P(("latent", "tok")),
        P(("latent", "tok"), "sub"),
        P("sub"),
        P("parts", None),
        P("parts"),
    )
    sizes = tuple(mesh.shape[name] for name in ("parts", "latent", "tok"))
    return jax.shard_map(
        functools.partial(per_device, sizes),
        mesh=mesh,
        in_specs=placed,
        out_specs=(P(("parts", "latent", "tok"), "sub"), P(("parts", "tok"), "latent")),
        check_vma=False,
    )
```

```python
import functools

import jax
import jax.numpy as jnp
from jax import lax
from jax.experimental import pallas as pl
from jax.experimental.pallas import tpu as pltpu
from jax.sharding import PartitionSpec as P

CAP = 6
PAD = 8
MESH = pl.DeviceIdType.MESH
BF16 = jnp.bfloat16
F32 = jnp.float32


def chunked(total, step):
    return [(at, min(step, total - at)) for at in range(0, total, step)]


def kernel(
    sizes, enc_parts, dec_parts,
    resid_hbm, enc_hbm, enc_bias_hbm, dec_hbm, dec_bias_hbm, spans_hbm, owners_hbm,
    recon_hbm, owned_hbm,
    resid, enc_bias, dec_bias_flat, dec_bias, spans, owners, recon, wenc, wdec, xg, xf, x2, mg, pe, pr, acts,
    ysend, yown, yrecv, csend, cown, crecv, psend, precv,
    small_sem, out_sem, wenc_sem, wdec_sem, gz_sem, g_sem, m_sem, e_sem, a_sem, c_sem, p_sem,
):
    n_p, n_l, n_t = sizes
    p, l, t, s = (lax.axis_index(name) for name in ("parts", "latent", "tok", "sub"))
    rows = resid.shape[0]
    half = acts.shape[1]
    total_rows = n_p * n_l * n_t * rows
    part_rows = n_l * n_t * rows

    def at(dp=0, dl=0, dt=0, ds=0):
        return (
            lax.rem(p + dp, n_p), lax.rem(l + dl, n_l), lax.rem(t + dt, n_t), lax.rem(s + ds, 2)
        )

    sent = []

    def send(src, dst, sems, index, device):
        copy = pltpu.make_async_remote_copy(
            src_ref=src, dst_ref=dst, send_sem=sems.at[(0,) + index],
            recv_sem=sems.at[(1,) + index], device_id=device, device_id_type=MESH,
        )
        copy.start()
        sent.append(copy)
        return copy

    base = pl.multiple_of(p * half, half)
    small = [
        pltpu.make_async_copy(src, dst, small_sem.at[j])
        for j, (src, dst) in enumerate((
            (resid_hbm, resid),
            (dec_bias_hbm, dec_bias_flat),
            (spans_hbm, spans),
            (owners_hbm, owners),
            (enc_bias_hbm.at[:, pl.ds(base, half)], enc_bias),
        ))
    ]
    for copy in small:
        copy.start()

    enc_copies = []
    for j, (start, width) in enumerate(enc_parts):
        copy = pltpu.make_async_copy(
            enc_hbm.at[:, pl.ds(pl.multiple_of(base + start, 128), width)],
            wenc.at[:, pl.ds(start, width)], wenc_sem.at[j],
        )
        copy.start(priority=1)
        enc_copies.append(copy)

    barrier = pltpu.get_barrier_semaphore()
    peers = [at(ds=1)]
    peers += [at(dl=k) for k in range(1, n_l)]
    peers += [at(dp=a, dt=b) for a in range(n_p) for b in range(n_t) if a or b]
    for peer in peers:
        pl.semaphore_signal(barrier, inc=1, device_id=peer, device_id_type=MESH)

    for copy in small:
        copy.wait()
    dec_bias[...] = dec_bias_flat[...].reshape(dec_bias.shape)

    xg[t, p, l] = (resid[...].astype(F32) - dec_bias[...]).astype(BF16)

    docs = spans.shape[0]
    row_i = lax.broadcasted_iota(jnp.int32, (docs, docs), 0)
    col_i = lax.broadcasted_iota(jnp.int32, (docs, docs), 1)
    across = jnp.broadcast_to(owners[...], (docs, docs))
    down = jnp.sum(jnp.where(row_i == col_i, across, 0), axis=1, keepdims=True)
    same = jnp.where((down == across) & (row_i < col_i), 1, 0)
    slots = jnp.sum(same, axis=0, keepdims=True)
    target = owners[...] * PAD + slots
    select = target == lax.broadcasted_iota(jnp.int32, (n_t * PAD, docs), 0)
    member = jnp.dot(
        jnp.where(select, 1.0, 0.0).astype(BF16), spans[...].astype(F32).astype(BF16),
        preferred_element_type=F32,
    )
    place = lax.broadcasted_iota(jnp.int32, (part_rows, total_rows), 1)
    source = lax.broadcasted_iota(jnp.int32, (part_rows, total_rows), 0)
    r_at = lax.rem(place, rows)
    l_at = lax.rem(lax.div(place, rows), n_l)
    p_at = lax.rem(lax.div(place, rows * n_l), n_p)
    t_at = lax.div(place, rows * n_l * n_p)
    wanted = jnp.where(p_at == p, (l_at * n_t + t_at) * rows + r_at, -1)
    mg[p] = jnp.dot(
        member.astype(BF16), jnp.where(source == wanted, 1.0, 0.0).astype(BF16),
        preferred_element_type=F32,
    )

    pl.semaphore_wait(barrier, len(peers))

    others = [(a, b) for a in range(n_p) for b in range(n_t) if a or b]

    def spread_rows(k, came):
        ref = xg.at[t, p, came]
        return [send(ref, ref, g_sem, (k, a, b), at(dp=a, dt=b)) for a, b in others]

    z_copies = [
        send(xg.at[t, p, l], xg.at[t, p, l], gz_sem, (k - 1,), at(dl=k)) for k in range(1, n_l)
    ]
    g_copies = spread_rows(0, l)
    m_copies = [send(mg.at[p], mg.at[p], m_sem, (k - 1,), at(dp=k)) for k in range(1, n_p)]
    dec_copies = []
    for j, (start, width) in enumerate(dec_parts):
        copy = pltpu.make_async_copy(
            dec_hbm.at[pl.ds(base, half), pl.ds(start, width)],
            wdec.at[:, pl.ds(start, width)], wdec_sem.at[j],
        )
        copy.start(priority=1)
        dec_copies.append(copy)
    for k, copy in enumerate(z_copies, 1):
        copy.wait_recv()
        g_copies += spread_rows(k, lax.rem(l + n_l - k, n_l))
    for copy in g_copies:
        copy.wait_recv()
    block = 0
    for a in range(n_t):
        for b in range(n_p):
            for c in range(n_l):
                xf[pl.ds(block * rows, rows), :] = xg[a, b, c].astype(F32)
                block += 1
    x2[...] = xf[...].astype(BF16)

    e_copies = []
    for j, (start, width) in enumerate(enc_parts):
        cols = pl.ds(start, width)
        enc_copies[j].wait()
        pe[:, cols] = jnp.dot(x2[...], wenc[:, cols], preferred_element_type=F32)
        e_copies.append(send(pe.at[:, cols], pr.at[:, cols], e_sem, (j,), at(ds=1)))

    def make_acts(j):
        start, width = enc_parts[j]
        cols = pl.ds(start, width)
        e_copies[j].wait_recv()
        acts[:, cols] = jnp.maximum(pe[:, cols] + pr[:, cols] + enc_bias[:, cols], 0.0).astype(BF16)

    a_copies, c_copies = {}, {}

    def decode(c):
        start, width = dec_parts[c]
        cols = pl.ds(start, width)
        dec_copies[c].wait()
        if c == 0:
            y = None
            for j, (k0, kw) in enumerate(enc_parts):
                make_acts(j)
                term = jnp.dot(
                    acts[:, pl.ds(k0, kw)], wdec[pl.ds(k0, kw), cols], preferred_element_type=F32
                )
                y = term if y is None else y + term
        else:
            y = jnp.dot(acts[...], wdec[:, cols], preferred_element_type=F32)
        tall = n_l * rows
        for a in range(n_t * n_p):
            piece = y[a * tall:(a + 1) * tall]
            ysend[a, :, cols] = piece.astype(BF16)
            yown[a, :, cols] = piece
        a_copies[c] = []
        for k, (a, b) in enumerate(others):
            peer = at(dp=a, dt=b)
            theirs = ysend.at[peer[2] * n_p + peer[0], :, cols]
            a_copies[c].append(send(theirs, yrecv.at[k, :, cols], a_sem, (c, k), peer))

    def sum_xy(c):
        start, width = dec_parts[c]
        cols = pl.ds(start, width)
        total = yown[t * n_p + p, :, cols]
        for k, copy in enumerate(a_copies[c]):
            copy.wait_recv()
            total += yrecv[k, :, cols].astype(F32)
        for a in range(n_l):
            piece = total[a * rows:(a + 1) * rows]
            csend[a, :, cols] = piece.astype(BF16)
            cown[a, :, cols] = piece
        c_copies[c] = []
        for k in range(1, n_l):
            peer = at(dl=k)
            c_copies[c].append(
                send(csend.at[peer[1], :, cols], crecv.at[k - 1, :, cols], c_sem, (c, k - 1), peer)
            )

    def sum_z(c):
        start, width = dec_parts[c]
        cols = pl.ds(start, width)
        total = cown[l, :, cols]
        for k, copy in enumerate(c_copies[c]):
            copy.wait_recv()
            total += crecv[k, :, cols].astype(F32)
        recon[:, cols] = (total + dec_bias[:, cols]).astype(BF16)

    def pool():
        for copy in m_copies:
            copy.wait_recv()
        spread = jnp.concatenate([mg[a] for a in range(n_p)], axis=0)
        counts = jnp.maximum(jnp.sum(spread, axis=1, keepdims=True), 1.0)
        pooled = jnp.dot(spread.astype(BF16), acts[...], preferred_element_type=F32) / counts
        for a in range(n_p * n_t):
            psend[a] = pooled[a * PAD:(a + 1) * PAD].astype(BF16)
        mine = p * n_t + t
        precv[mine] = psend[mine]
        copies = []
        for a, b in others:
            peer = at(dp=a, dt=b)
            theirs = psend.at[peer[0] * n_t + peer[2]]
            copies.append(send(theirs, precv.at[mine], p_sem, (a, b), peer))
        return copies

    steps = len(dec_parts)
    pool_copies, out_copies = [], []
    for c in range(steps):
        decode(c)
        if c == steps - 1:
            pool_copies = pool()
    for c in range(steps):
        sum_xy(c)
    for copy in pool_copies:
        copy.wait_recv()
    for a in range(n_p):
        for b in range(n_t):
            out_copies.append(pltpu.make_async_copy(
                precv.at[a * n_t + b],
                owned_hbm.at[:, pl.ds((b * n_p + a) * half, half)],
                out_sem.at[1 + a * n_t + b],
            ))
            out_copies[-1].start()
    for c in range(steps):
        sum_z(c)
    out_copies.append(pltpu.make_async_copy(recon, recon_hbm, out_sem.at[0]))
    out_copies[-1].start()
    for copy in sent:
        copy.wait_send()
    for copy in out_copies:
        copy.wait()


def per_device(sizes, resid, enc_weight, enc_bias, dec_weight, dec_bias, spans, owners):
    n_p, n_l, n_t = sizes
    rows, width = resid.shape
    half = enc_weight.shape[1] // n_p
    total = rows * n_p * n_l * n_t
    enc_parts = chunked(half, 1024)
    dec_parts = chunked(width, 512)
    hbm = pl.BlockSpec(memory_space=pl.ANY)
    dma = pltpu.SemaphoreType.DMA
    planes, tall = n_t * n_p, n_l * rows
    more = lambda n: max(n - 1, 1)
    steps = len(dec_parts)
    out_shape = (
        jax.ShapeDtypeStruct((rows, width), BF16),
        jax.ShapeDtypeStruct((PAD, half * n_p * n_t), BF16),
    )
    recon, owned = pl.pallas_call(
        functools.partial(kernel, sizes, enc_parts, dec_parts),
        out_shape=out_shape,
        in_specs=[hbm] * 7,
        out_specs=(hbm, hbm),
        scratch_shapes=[
            pltpu.VMEM((rows, width), BF16),
            pltpu.VMEM((1, half), F32),
            pltpu.VMEM((width,), F32),
            pltpu.VMEM((1, width), F32),
            pltpu.VMEM(spans.shape, jnp.int32),
            pltpu.VMEM((1, owners.shape[0]), jnp.int32),
            pltpu.VMEM((rows, width), BF16),
            pltpu.VMEM((width, half), BF16),
            pltpu.VMEM((half, width), BF16),
            pltpu.VMEM((n_t, n_p, n_l, rows, width), BF16),
            pltpu.VMEM((total, width), F32),
            pltpu.VMEM((total, width), BF16),
            pltpu.VMEM((n_p, n_t * PAD, total), F32),
            pltpu.VMEM((total, half), F32),
            pltpu.VMEM((total, half), F32),
            pltpu.VMEM((total, half), BF16),
            pltpu.VMEM((planes, tall, width), BF16),
            pltpu.VMEM((planes, tall, width), F32),
            pltpu.VMEM((more(planes), tall, width), BF16),
            pltpu.VMEM((n_l, rows, width), BF16),
            pltpu.VMEM((n_l, rows, width), F32),
            pltpu.VMEM((more(n_l), rows, width), BF16),
            pltpu.VMEM((n_p * n_t, PAD, half), BF16),
            pltpu.VMEM((n_p * n_t, PAD, half), BF16),
            dma((5,)),
            dma((1 + planes,)),
            dma((len(enc_parts),)),
            dma((steps,)),
            dma((2, more(n_l))),
            dma((2, n_l, n_p, n_t)),
            dma((2, more(n_p))),
            dma((2, len(enc_parts))),
            dma((2, steps, more(planes))),
            dma((2, steps, more(n_l))),
            dma((2, n_p, n_t)),
        ],
        compiler_params=pltpu.CompilerParams(
            collective_id=0, has_side_effects=True, vmem_limit_bytes=58 * 1024 * 1024
        ),
        cost_estimate=pl.CostEstimate(
            flops=4 * total * width * half, bytes_accessed=4 * width * half, transcendentals=0
        ),
    )(
        resid, enc_weight, enc_bias[None, :], dec_weight, dec_bias, spans, owners[None, :]
    )
    return recon, owned[:CAP]


def solution(mesh):
    placed = (
        P(("parts", "latent", "tok"), "sub"),
        P("sub", ("latent", "tok")),
        P(("latent", "tok")),
        P(("latent", "tok"), "sub"),
        P("sub"),
        P("parts", None),
        P("parts"),
    )
    sizes = tuple(mesh.shape[name] for name in ("parts", "latent", "tok"))
    return jax.shard_map(
        functools.partial(per_device, sizes),
        mesh=mesh,
        in_specs=placed,
        out_specs=(P(("parts", "latent", "tok"), "sub"), P(("parts", "tok"), "latent")),
        check_vma=False,
    )
```
